32 devices in a mesh: groups: 2 (over y), rows: 4 (over z), dates: 2 (over x), cols: 2 (over core).
Axes of the slice: x: 2, y: 2, z: 4, core: 2. Of those that a mesh axis runs over, the one named last changes fastest.
Arguments:
- images: bfloat16 [4, 13, 64, 1024], P('dates', None, ('groups', 'rows'), 'cols'), parts along dimension 2, may hold values from -6 to 6
- cloud_mask: int32 [4, 64, 1024], P(None, ('groups', 'rows', 'dates'), 'cols'), parts along dimension 1, may hold values 0 or 1
- counts: int32 [64, 1024], P(('groups', 'rows', 'dates'), 'cols'), parts along dimension 0, may hold values from 1 to 4
- day_of_year: int32 [8], P('groups'), parts along dimension 0, may hold values from 0 to 365
- w_first: bfloat16 [3, 3, 13, 128], replicated, may hold values from -0.5 to 0.5
- b_first: float32 [128], replicated, may hold values from -1.75 to 1.75
- w_second: bfloat16 [3, 3, 128, 128], replicated, may hold values from -0.25 to 0.25
- b_second: float32 [128], replicated, may hold values from -1.75 to 1.75
- w_third: bfloat16 [3, 3, 128, 128], replicated, may hold values from -0.25 to 0.25
- b_third: float32 [128], replicated, may hold values from -1.75 to 1.75
- w_in: bfloat16 [128, 256], replicated, may hold values from -0.75 to 0.75
- w_key: bfloat16 [256, 64], replicated, may hold values from -0.375 to 0.375
- master_query: float32 [16, 4], replicated, may hold values from -8 to 8
- w_mlp: bfloat16 [256, 128], replicated, may hold values from -0.5 to 0.5
- b_mlp: float32 [128], replicated, may hold values from -1.75 to 1.75
- w_dec: bfloat16 [3, 3, 128, 128], replicated, may hold values from -0.25 to 0.25
- b_dec: float32 [128], replicated, may hold values from -1.75 to 1.75
- w_out: bfloat16 [13, 128], replicated, may hold values from -0.75 to 0.75
- b_out: float32 [13], replicated, may hold values from -3 to 3
Outputs:
- prediction: float32 [13, 64, 1024], P(None, ('groups', 'rows', 'dates'), 'cols'), parts along dimension 1
The draws below stay inside these ranges and needn't reach their ends.
There are 2 independent parts, one for each index of `groups`. The reference program is written for one: setup_inputs(seed, part) draws one part's arguments, and reference() takes and returns one part's arrays. A program takes and returns all parts, laid end to end along the dimension named above; an argument that names none is the same for every part. Nothing has to cross between parts.
All inputs are finite; a program needn't handle non-finite values. No bound on the sum of `cloud_mask` on one device may be relied on, other than what follows from the above.
Results may differ from the reference program's by a relative error of at most 0.012.
Values may be sent and summed in bfloat16 or wider, within the bound.
A program may use at most 64 MiB of HBM per device.

```python
import math
import jax
import jax.numpy as jnp
from jax import lax

BANDS = 13
CHAN = 128
DMODEL = 256
HEADS = 16
DK = 4
RS = 8
T_SIZE = 4
H = 32
W = 1024


def plant(values, rng, low, high):
    extent = values.shape
    spot = [jax.random.randint(jax.random.fold_in(rng, axis), (), 0, extent[axis]) for axis in range(len(extent))]
    values = values.at[tuple(spot)].set(low)
    longest = extent.index(max(extent))
    spot[longest] = (spot[longest] + 1) % extent[longest]
    return values.at[tuple(spot)].set(high)


def levels(rng, dims, pieces, smallest, top_value):
    def one(axis_at, parts):
        steps = jax.random.uniform(jax.random.fold_in(jax.random.fold_in(rng, 6), axis_at), (parts,), jnp.float32, smallest / len(pieces), top_value / len(pieces))
        return jnp.repeat(jnp.exp(steps), dims[axis_at] // parts).reshape((-1,) + (1,) * (len(dims) - axis_at - 1))

    factor_of = one(*pieces[0])
    for cut in pieces[1:]:
        factor_of = factor_of * one(*cut)
    return factor_of


def centred(key, extent, scale, reach, cuts=(), kind=jnp.bfloat16):
    values = jax.random.normal(key, extent, jnp.float32) * scale
    if len(cuts) > 0:
        values = levels(key, extent, cuts, -0.22, 0.18) * values
    return jnp.clip(values, min=-reach, max=reach).astype(kind)


def setup_inputs(seed: int = 0, part: int = 0) -> dict:
    streams_of = jax.random.split(jax.random.key(seed), 20)
    own_keys = jax.random.split(jax.random.fold_in(streams_of[19], part), 20)
    images = centred(own_keys[0], (T_SIZE, BANDS, H, W), 1.0, 6.0, ((0, 2), (2, 4), (3, 2)))
    cloud_mask = plant((jax.random.randint(own_keys[1], (T_SIZE, H, W), 0, 3) < 1).astype(jnp.int32), jax.random.fold_in(own_keys[1], 1), 0, 1)
    counts = plant(jax.random.randint(own_keys[2], (H, W), 1, T_SIZE + 1), jax.random.fold_in(own_keys[2], 1), 1, T_SIZE).astype(jnp.int32)
    day_of_year = plant(jax.random.randint(own_keys[3], (T_SIZE,), 0, 366), jax.random.fold_in(own_keys[3], 1), 0, 365).astype(jnp.int32)
    w_first = centred(streams_of[4], (3, 3, BANDS, CHAN), (9 * BANDS) ** -0.5, 0.5)
    b_first = centred(streams_of[5], (CHAN,), 0.3, 1.75, (), jnp.float32)
    w_second = centred(streams_of[6], (3, 3, CHAN, CHAN), (4.5 * CHAN) ** -0.5, 0.25)
    b_second = centred(streams_of[7], (CHAN,), 0.3, 1.75, (), jnp.float32)
    w_third = centred(streams_of[8], (3, 3, CHAN, CHAN), (4.5 * CHAN) ** -0.5, 0.25)
    b_third = centred(streams_of[9], (CHAN,), 0.3, 1.75, (), jnp.float32)
    w_in = centred(streams_of[10], (CHAN, DMODEL), (CHAN / 2) ** -0.5, 0.75)
    w_key = centred(streams_of[11], (DMODEL, HEADS * DK), DMODEL ** -0.5, 0.375)
    master_query = centred(streams_of[12], (HEADS, DK), 1.5, 8.0, (), jnp.float32)
    w_mlp = centred(streams_of[13], (DMODEL, CHAN), (DMODEL / 2) ** -0.5, 0.5)
    b_mlp = centred(streams_of[14], (CHAN,), 0.3, 1.75, (), jnp.float32)
    w_dec = centred(streams_of[15], (3, 3, CHAN, CHAN), (4.5 * CHAN) ** -0.5, 0.25)
    b_dec = centred(streams_of[16], (CHAN,), 0.3, 1.75, (), jnp.float32)
    w_out = centred(streams_of[17], (BANDS, CHAN), (CHAN / 2) ** -0.5, 0.75)
    b_out = centred(streams_of[18], (BANDS,), 0.5, 3.0, (), jnp.float32)
    return {"images": images, "cloud_mask": cloud_mask, "counts": counts, "day_of_year": day_of_year, "w_first": w_first, "b_first": b_first, "w_second": w_second, "b_second": b_second, "w_third": w_third, "b_third": b_third, "w_in": w_in, "w_key": w_key, "master_query": master_query, "w_mlp": w_mlp, "b_mlp": b_mlp, "w_dec": w_dec, "b_dec": b_dec, "w_out": w_out, "b_out": b_out}


def conv_same(source, kernel, offset):
    result = lax.conv_general_dilated(source.astype(jnp.float32), kernel.astype(jnp.float32), (1, 1), ((1, 1), (1, 1)), dimension_numbers=('NCHW', 'HWIO', 'NCHW'), precision=lax.Precision.HIGHEST)
    return jax.nn.relu(result + offset.astype(jnp.float32)[None, :, None, None]).astype(jnp.bfloat16)

def positions(day_of_year):
    channel = jnp.arange(DMODEL // 2).astype(jnp.float32)
    frequency = jnp.power(jnp.float32(1000.0), -2.0 * channel / DMODEL)
    angle_table = day_of_year.astype(jnp.float32)[:, None] * frequency[None, :]
    return jnp.stack([jnp.sin(angle_table), jnp.cos(angle_table)], axis=-1).reshape(day_of_year.shape[0], DMODEL)

def attend(features, cloud_mask, counts, position, w_in, w_key, master_query, w_mlp, b_mlp):
    dates = features.shape[0]
    pixels = features.shape[2]
    projected = jnp.einsum('tcp,cd->tdp', features.astype(jnp.float32), w_in.astype(jnp.float32))
    projected = (projected + position[:, :, None]).astype(jnp.bfloat16)
    keyed = jnp.einsum('tdp,dk->tkp', projected.astype(jnp.float32), w_key.astype(jnp.float32))
    keyed = keyed.reshape(dates, HEADS, DK, pixels)
    raw_scores = lax.optimization_barrier(jnp.sum(keyed * master_query[None, :, :, None], axis=2)) / math.sqrt(DK)
    scores = 8.0 * jnp.tanh(raw_scores / 8.0) - 4.0 * cloud_mask.astype(jnp.float32)[:, None, :]
    usable = (jnp.arange(dates)[:, None] < counts[None, :]).astype(jnp.float32)
    weights = jnp.exp(scores) * usable[:, None, :]
    attention = (weights / lax.optimization_barrier(jnp.sum(weights, axis=0, keepdims=True))).astype(jnp.bfloat16)
    grouped = projected.reshape(dates, HEADS, DMODEL // HEADS, pixels)
    pooled = jnp.einsum('thp,thgp->hgp', attention.astype(jnp.float32), grouped.astype(jnp.float32))
    pooled = pooled.reshape(DMODEL, pixels).astype(jnp.bfloat16)
    mixed_out = jnp.einsum('dp,dc->cp', pooled.astype(jnp.float32), w_mlp.astype(jnp.float32))
    return jax.nn.relu(mixed_out + b_mlp[:, None]).astype(jnp.bfloat16)

def reference(images, cloud_mask, counts, day_of_year, w_first, b_first, w_second, b_second, w_third, b_third, w_in, w_key, master_query, w_mlp, b_mlp, w_dec, b_dec, w_out, b_out):

    def encode_date(image):
        layer_one = conv_same(image[None], w_first, b_first)
        layer_two = conv_same(layer_one, w_second, b_second)
        return conv_same(layer_two, w_third, b_third)[0]
    encoded = lax.map(encode_date, images)
    position = positions(day_of_year)
    blocks = H // RS
    feature_blocks = encoded.reshape(T_SIZE, CHAN, blocks, RS * W).transpose(2, 0, 1, 3)
    cloud_blocks = cloud_mask.reshape(T_SIZE, blocks, RS * W).transpose(1, 0, 2)
    count_blocks = counts.reshape(blocks, RS * W)

    def one_block(items):
        return attend(items[0], items[1], items[2], position, w_in, w_key, master_query, w_mlp, b_mlp)
    mixed_out = lax.map(one_block, (feature_blocks, cloud_blocks, count_blocks))
    mixed_out = mixed_out.transpose(1, 0, 2).reshape(CHAN, H, W)
    decoded = conv_same(mixed_out[None], w_dec, b_dec)[0]
    prediction = jnp.einsum('oc,chw->ohw', w_out.astype(jnp.float32), decoded.astype(jnp.float32))
    return prediction + b_out[:, None, None]
```

```python
import functools
import math

import jax
import jax.numpy as jnp
import numpy as np
from jax import lax
from jax.experimental import pallas as pl
from jax.experimental.pallas import tpu as pltpu
from jax.sharding import PartitionSpec as P

SIDE = 16
BF = jnp.bfloat16
F32 = jnp.float32


def positions(day_of_year, width_model):
    channel = jnp.arange(width_model // 2).astype(F32)
    frequency = jnp.power(F32(1000.0), -2.0 * channel / width_model)
    angle_table = day_of_year.astype(F32)[:, None] * frequency[None, :]
    return jnp.stack([jnp.sin(angle_table), jnp.cos(angle_table)], axis=-1).reshape(
        day_of_year.shape[0], width_model
    )


def dot(a, b):
    return jnp.dot(a, b, preferred_element_type=F32)


def dot_tn(a, b):
    return lax.dot_general(a, b, (((0,), (0,)), ((), ())), preferred_element_type=F32)


def dot_nt(a, b):
    return lax.dot_general(a, b, (((1,), (1,)), ((), ())), preferred_element_type=F32)


def kernel(
    cfg,
    img_ref,
    mk_ref,
    perm_ref,
    pos_ref,
    w1_ref,
    b1_ref,
    w2_ref,
    b2_ref,
    w3_ref,
    b3_ref,
    win_ref,
    wkey_ref,
    q_ref,
    ex_ref,
    bsel_ref,
    wmlp_ref,
    bmlp_ref,
    wdec_ref,
    bdec_ref,
    wout_ref,
    bout_ref,
    out_ref,
    mine,
    xbuf,
    mkb,
    xw,
    s1,
    s2,
    s3,
    enc,
    pa,
    k1,
    k2,
    k3,
    kd,
    ws,
    sel,
    send_sem,
    recv_sem,
    mask_send,
    mask_recv,
):
    (R, D, dl, own, strip, wdev, heads, model, bands) = cfg
    T = D * dl
    L = T * heads
    M = wdev + 2 * SIDE
    half = strip // 2
    r = lax.axis_index("rows")
    d = lax.axis_index("dates")
    c = lax.axis_index("cols")
    cp = 1 - c
    f = r * D + d
    height = R * strip

    mine[...] = jnp.zeros_like(mine)
    xbuf[...] = jnp.zeros_like(xbuf)
    mkb[...] = jnp.zeros_like(mkb)

    barrier = pltpu.get_barrier_semaphore()

    def greet(rr, others_only):
        for k in range(D):
            for other in range(2):
                if others_only and k == 0 and other == 0:
                    continue
                pl.semaphore_signal(
                    barrier,
                    inc=1,
                    device_id={
                        "rows": rr,
                        "dates": lax.rem(d + k, D),
                        "cols": cp if other else c,
                    },
                    device_id_type=pl.DeviceIdType.MESH,
                )

    greet(r, True)

    @pl.when(r > 0)
    def _():
        greet(r - 1, False)

    @pl.when(r < R - 1)
    def _():
        greet(r + 1, False)

    turned = dot_tn(img_ref[...], perm_ref[...]).astype(BF)
    for hb in range(2):
        mine[hb] = turned[:, hb * 128 : (hb + 1) * 128]
        xbuf[d, 1 + hb, SIDE : SIDE + wdev, :] = turned[:, hb * 128 : (hb + 1) * 128]
    mkb[1 : 1 + own, :, 128 : 128 + wdev] = mk_ref[...]

    src_side = pl.multiple_of(cp * (wdev - SIDE), SIDE)
    dst_side = pl.multiple_of(c * (wdev + SIDE), SIDE)
    msrc_side = pl.multiple_of(128 + cp * (wdev - 128), 128)
    mdst_side = pl.multiple_of(c * (wdev + 128), 128)

    def image_copy(kind, src_d, dst_d, rr, sd):
        side = kind % 2
        where = kind // 2
        if where == 0:
            blocks, dst_blocks = pl.ds(0, 2), pl.ds(1, 2)
        elif where == 1:
            blocks, dst_blocks = pl.ds(0, 1), pl.ds(3, 1)
        else:
            blocks, dst_blocks = pl.ds(1, 1), pl.ds(0, 1)
        if side:
            a, b = pl.ds(src_side, SIDE), pl.ds(dst_side, SIDE)
        else:
            a, b = pl.ds(0, wdev), pl.ds(SIDE, wdev)
        return pltpu.make_async_remote_copy(
            src_ref=mine.at[blocks, a, :],
            dst_ref=xbuf.at[src_d, dst_blocks, b, :],
            send_sem=send_sem.at[kind * D + sd],
            recv_sem=recv_sem.at[kind * D + src_d],
            device_id={"rows": rr, "dates": dst_d, "cols": cp if side else c},
            device_id_type=pl.DeviceIdType.MESH,
        )

    def mask_copy(kind, to):
        side = kind % 2
        where = kind // 2
        if where == 0:
            a, b = pl.ds(1, own), pl.ds(1, own)
        elif where == 1:
            a, b = pl.ds(1, 1), pl.ds(own + 1, 1)
        else:
            a, b = pl.ds(own, 1), pl.ds(0, 1)
        if side:
            x, y = pl.ds(msrc_side, 128), pl.ds(mdst_side, 128)
        else:
            x, y = pl.ds(128, wdev), pl.ds(128, wdev)
        return pltpu.make_async_remote_copy(
            src_ref=mkb.at[a, :, x],
            dst_ref=mkb.at[b, :, y],
            send_sem=mask_send.at[kind],
            recv_sem=mask_recv.at[kind],
            device_id={"rows": to // D, "dates": lax.rem(to, D), "cols": cp if side else c},
            device_id_type=pl.DeviceIdType.MESH,
        )

    def needs_next(q):
        return own * q + own + 4 > strip

    def needs_prev(q):
        return own * q < 4

    greeted = 2 * D - 1 + 2 * D * ((r > 0).astype(jnp.int32) + (r < R - 1).astype(jnp.int32))
    pl.semaphore_wait(barrier, greeted)

    def sends(act):
        @pl.when(r > 0)
        def _():
            for k in range(D):
                to = lax.rem(d + k, D)

                @pl.when(needs_next(to))
                def _():
                    act(image_copy(2, d, to, r - 1, k))
                    act(image_copy(3, d, to, r - 1, k))

        @pl.when(r < R - 1)
        def _():
            for k in range(D):
                to = lax.rem(d + k, D)

                @pl.when(needs_prev(to))
                def _():
                    act(image_copy(4, d, to, r + 1, k))
                    act(image_copy(5, d, to, r + 1, k))

        for k in range(D):
            to = lax.rem(d + k, D)
            act(image_copy(1, d, to, r, k))
            if k > 0:
                act(image_copy(0, d, to, r, k))
        act(mask_copy(1, f))

        @pl.when(f > 0)
        def _():
            act(mask_copy(2, f - 1))
            act(mask_copy(3, f - 1))

        @pl.when(f < R * D - 1)
        def _():
            act(mask_copy(4, f + 1))
            act(mask_copy(5, f + 1))

    sends(lambda copy: copy.start())

    def arrived(k):
        source = lax.rem(d + k, D)
        image_copy(1, source, d, r, k).wait_recv()
        if k > 0:
            image_copy(0, source, d, r, k).wait_recv()

        @pl.when((r < R - 1) & needs_next(d))
        def _():
            image_copy(2, source, d, r, k).wait_recv()
            image_copy(3, source, d, r, k).wait_recv()

        @pl.when((r > 0) & needs_prev(d))
        def _():
            image_copy(4, source, d, r, k).wait_recv()
            image_copy(5, source, d, r, k).wait_recv()

    k1[...] = jnp.zeros_like(k1)
    for off in range(4):
        for dy in range(3):
            for dx in range(3):
                for o in range(2):
                    row = 2 * off + o + dy
                    at = (row // 8) * 384 + dx * 128 + (row % 8) * 16
                    k1[off, at : at + 16, o * 128 : (o + 1) * 128] = w1_ref[dy, dx]
    for w_ref, k_ref in ((w2_ref, k2), (w3_ref, k3), (wdec_ref, kd)):
        k_ref[...] = jnp.zeros_like(k_ref)
        for dy in range(3):
            for dx in range(3):
                for o in range(2):
                    at = (o + dy) * 384 + dx * 128
                    k_ref[at : at + 128, o * 128 : (o + 1) * 128] = w_ref[dy, dx]

    full = lax.dot_general(
        wkey_ref[...].astype(F32),
        q_ref[...],
        (((1,), (0,)), ((), ())),
        precision=lax.Precision.HIGHEST,
        preferred_element_type=F32,
    )
    high = full.astype(BF).astype(F32)
    lane = lax.broadcasted_iota(jnp.int32, full.shape, 1)
    both = jnp.where(lane < L, high, full - high)
    for t in range(T):
        mine_t = (lane % L) // heads == t
        ws[t * model : (t + 1) * model, :] = jnp.where(mine_t, both, 0.0).astype(BF)

    kk = lax.broadcasted_iota(jnp.int32, (512, 256), 0)
    nn = lax.broadcasted_iota(jnp.int32, (512, 256), 1)
    same = ((kk // 128) * 4 + (kk % 64) // 16 == d * own + nn // 16) & (kk % 16 == nn % 16)
    for p in range(dl):
        sel[p] = jnp.where(same & ((kk % 128) // 64 == p), 1.0, 0.0).astype(BF)

    px = lax.broadcasted_iota(jnp.int32, (M, 128), 0)
    at_col = px + (c * wdev - SIDE)
    inside = (at_col >= 0) & (at_col < 2 * wdev)
    col_mask = jnp.where(inside, 1.0, 0.0).astype(F32)
    first_row = r * strip + d * own

    def row_mask(rel):
        at = first_row + rel
        ok = ((at >= 0) & (at < height)).astype(F32)
        return ok

    def spread(y, into, base, rel):
        y = y * (col_mask * row_mask(rel))
        into[:, pl.ds(base, 128)] = pltpu.roll(y, 1, 0).astype(BF)
        into[:, pl.ds(base + 128, 128)] = y.astype(BF)
        into[:, pl.ds(base + 256, 128)] = pltpu.roll(y, M - 1, 0).astype(BF)

    def one_date(i, carry):
        t = lax.rem(d * dl + i, T)
        source = t // dl
        par = lax.rem(t, dl)
        window = dot(xbuf[source, 0], sel[par, 0:128, :])
        for b in range(1, 4):
            window = window + dot(xbuf[source, b], sel[par, b * 128 : (b + 1) * 128, :])
        for h in range(2):
            part = window[:, h * 128 : (h + 1) * 128]
            xw[:, h * 384 : h * 384 + 128] = pltpu.roll(part, 1, 0).astype(BF)
            xw[:, h * 384 + 128 : h * 384 + 256] = part.astype(BF)
            xw[:, h * 384 + 256 : h * 384 + 384] = pltpu.roll(part, M - 1, 0).astype(BF)
        for j in range((own + 6) // 2):
            at = (j // 4) * 384
            if j % 4 == 3:
                y = dot(xw[...], k1[3])
            else:
                y = dot(xw[:, at : at + 384], k1[j % 4, 0:384, :])
            for o in range(2):
                v = jnp.maximum(y[:, o * 128 : (o + 1) * 128] + b1_ref[...], 0.0)
                spread(v, s1, (2 * j + o) * 384, 2 * j + o - 3)
        for j in range((own + 4) // 2):
            y = dot(s1[:, j * 768 : j * 768 + 1536], k2[...])
            for o in range(2):
                v = jnp.maximum(y[:, o * 128 : (o + 1) * 128] + b2_ref[...], 0.0)
                spread(v, s2, (2 * j + o) * 384, 2 * j + o - 2)
        for j in range((own + 2) // 2):
            y = dot(s2[:, j * 768 : j * 768 + 1536], k3[...])
            for o in range(2):
                v = jnp.maximum(y[:, o * 128 : (o + 1) * 128] + b3_ref[...], 0.0)
                enc[t, :, (2 * j + o) * 128 : (2 * j + o + 1) * 128] = v.astype(BF)
        return carry

    for k in range(D):
        arrived(k)
        lax.fori_loop(k * dl, (k + 1) * dl, one_date, 0)

    mask_copy(1, f).wait_recv()

    @pl.when(f < R * D - 1)
    def _():
        mask_copy(2, f).wait_recv()
        mask_copy(3, f).wait_recv()

    @pl.when(f > 0)
    def _():
        mask_copy(4, f).wait_recv()
        mask_copy(5, f).wait_recv()

    def one_row(i, carry):
        at = pl.multiple_of(i * 128, 128)
        for t in range(T):
            v = dot(enc[t, :, pl.ds(at, 128)], win_ref[...]) + pos_ref[t : t + 1, :]
            pa[:, t * model : (t + 1) * model] = v.astype(BF)
        z = dot(pa[...], ws[...])
        raw = z + pltpu.roll(z, L, 1)
        extra = dot_tn(mkb[i], bsel_ref[...])[128 - SIDE : 128 + wdev + SIDE]
        w = jnp.exp(8.0 * jnp.tanh(raw * 0.125) + extra)
        total = w
        step = heads
        while step < L:
            total = total + pltpu.roll(total, step, 1)
            step *= 2
        att = (w / total).astype(BF)
        pooled = None
        for t in range(T):
            cols = slice(t * model, (t + 1) * model)
            term = dot(att, ex_ref[:, cols]) * pa[:, cols].astype(F32)
            pooled = term if pooled is None else pooled + term
        v = jnp.maximum(dot(pooled.astype(BF), wmlp_ref[...]) + bmlp_ref[...], 0.0)
        spread(v, s3, pl.multiple_of(i * 384, 128), i - 1)
        return carry

    lax.fori_loop(0, own + 2, one_row, 0)

    for j in range(own // 2):
        y = dot(s3[:, j * 768 : j * 768 + 1536], kd[...])
        for o in range(2):
            v = jnp.maximum(y[SIDE : SIDE + wdev, o * 128 : (o + 1) * 128] + bdec_ref[...], 0.0)
            res = dot_nt(wout_ref[...], v.astype(BF)) + bout_ref[...]
            out_ref[:, 2 * j + o, :] = res[0:bands]

    sends(lambda copy: copy.wait_send())


def on_device(
    axes,
    images,
    cloud_mask,
    counts,
    day_of_year,
    w_first,
    b_first,
    w_second,
    b_second,
    w_third,
    b_third,
    w_in,
    w_key,
    master_query,
    w_mlp,
    b_mlp,
    w_dec,
    b_dec,
    w_out,
    b_out,
):
    R, D = axes
    dl, bands, strip, wdev = images.shape
    own = counts.shape[0]
    T = cloud_mask.shape[0]
    heads, key_size = master_query.shape
    model = w_in.shape[1]
    L = T * heads
    M = wdev + 2 * SIDE
    chan = w_in.shape[0]
    cfg = (R, D, dl, own, strip, wdev, heads, model, bands)

    invalid = jnp.arange(T)[:, None, None] >= counts[None]
    mk = jnp.concatenate([cloud_mask.astype(BF), invalid.astype(BF)], axis=0)
    mk = jnp.pad(mk, ((0, 16 - 2 * T), (0, 0), (0, 0))).transpose(1, 0, 2)

    perm = np.zeros((dl * bands * strip, 256), np.float32)
    for p in range(dl):
        for ch in range(bands):
            for row in range(strip):
                lane = (row // 4) * 128 + p * 64 + (row % 4) * 16 + ch
                perm[(p * bands + ch) * strip + row, lane] = 1.0
    n = np.arange(2 * L)
    head_of = n % heads
    date_of = (n % L) // heads
    ex = np.zeros((2 * L, T * model), np.float32)
    for t in range(T):
        for m in range(model):
            ex[t * heads + m // (model // heads), t * model + m] = 1.0
    bsel = np.zeros((16, 2 * L), np.float32)
    for t in range(T):
        bsel[t, date_of == t] = -4.0
        bsel[T + t, date_of == t] = -1e30
    pick = (np.arange(heads * key_size)[:, None] // key_size == head_of[None, :]).astype(np.float32)
    q = master_query.reshape(heads * key_size, 1) * (pick / math.sqrt(key_size))

    args = (
        images.reshape(dl * bands * strip, wdev),
        mk,
        jnp.asarray(perm, BF),
        positions(day_of_year, model),
        jnp.pad(w_first, ((0, 0), (0, 0), (0, 16 - bands), (0, 0))),
        b_first[None],
        w_second,
        b_second[None],
        w_third,
        b_third[None],
        w_in,
        w_key,
        q,
        jnp.asarray(ex, BF),
        jnp.asarray(bsel, BF),
        w_mlp,
        b_mlp[None],
        w_dec,
        b_dec[None],
        jnp.pad(w_out, ((0, 16 - bands), (0, 0))),
        jnp.pad(b_out, (0, 16 - bands))[:, None],
    )
    return pl.pallas_call(
        functools.partial(kernel, cfg),
        out_shape=jax.ShapeDtypeStruct((bands, own, wdev), F32),
        in_specs=[pl.BlockSpec(memory_space=pltpu.VMEM)] * len(args),
        out_specs=pl.BlockSpec(memory_space=pltpu.VMEM),
        scratch_shapes=[
            pltpu.VMEM((2, wdev, 128), BF),
            pltpu.VMEM((D, 4, M, 128), BF),
            pltpu.VMEM((own + 2, 16, wdev + 256), BF),
            pltpu.VMEM((M, 768), BF),
            pltpu.VMEM((M, (own + 6) * 384), BF),
            pltpu.VMEM((M, (own + 4) * 384), BF),
            pltpu.VMEM((M, (own + 2) * 384), BF),
            pltpu.VMEM((T, M, (own + 2) * 128), BF),
            pltpu.VMEM((M, T * model), BF),
            pltpu.VMEM((4, 768, 256), BF),
            pltpu.VMEM((12 * chan, 2 * chan), BF),
            pltpu.VMEM((12 * chan, 2 * chan), BF),
            pltpu.VMEM((12 * chan, 2 * chan), BF),
            pltpu.VMEM((T * model, 2 * L), BF),
            pltpu.VMEM((dl, 512, 256), BF),
            pltpu.SemaphoreType.DMA((6 * D,)),
            pltpu.SemaphoreType.DMA((6 * D,)),
            pltpu.SemaphoreType.DMA((6,)),
            pltpu.SemaphoreType.DMA((6,)),
        ],
        compiler_params=pltpu.CompilerParams(
            collective_id=0, has_side_effects=True, vmem_limit_bytes=56 * 1024 * 1024
        ),
    )(*args)


def solution(mesh):
    placed = (
        P("dates", None, ("groups", "rows"), "cols"),
        P(None, ("groups", "rows", "dates"), "cols"),
        P(("groups", "rows", "dates"), "cols"),
        P("groups"),
    ) + (P(),) * 15
    return jax.shard_map(
        functools.partial(on_device, (mesh.shape["rows"], mesh.shape["dates"])),
        mesh=mesh,
        in_specs=placed,
        out_specs=P(None, ("groups", "rows", "dates"), "cols"),
        check_vma=False,
    )
```

```python
import functools
import math

import jax
import jax.numpy as jnp
import numpy as np
from jax import lax
from jax.experimental import pallas as pl
from jax.experimental.pallas import tpu as pltpu
from jax.sharding import PartitionSpec as P

SIDE = 16
BF = jnp.bfloat16
F32 = jnp.float32


def dot(a, b):
    return jnp.dot(a, b, preferred_element_type=F32)


def dot_tn(a, b):
    return lax.dot_general(a, b, (((0,), (0,)), ((), ())), preferred_element_type=F32)


def dot_nt(a, b):
    return lax.dot_general(a, b, (((1,), (1,)), ((), ())), preferred_element_type=F32)


def kernel(
    cfg,
    img_ref,
    cloud_ref,
    counts_ref,
    day_ref,
    freq_ref,
    perm_ref,
    w1_ref,
    b1_ref,
    w2_ref,
    b2_ref,
    w3_ref,
    b3_ref,
    win_ref,
    wkey_ref,
    query_ref,
    ex_ref,
    bsel_ref,
    wmlp_ref,
    bmlp_ref,
    wdec_ref,
    bdec_ref,
    wout_ref,
    out_ref,
    mine,
    xbuf,
    mkb,
    xw,
    s1,
    s2,
    s3,
    enc,
    pa,
    k1,
    k2,
    k3,
    kd,
    ws,
    sel,
    pos_ref,
    posr_ref,
    send_sem,
    recv_sem,
    mask_send,
    mask_recv,
):
    (R, D, dl, own, strip, wdev, heads, model, bands) = cfg
    T = D * dl
    L = T * heads
    M = wdev + 2 * SIDE
    half = strip // 2
    r = lax.axis_index("rows")
    d = lax.axis_index("dates")
    c = lax.axis_index("cols")
    cp = 1 - c
    f = r * D + d
    height = R * strip

    mine[...] = jnp.zeros_like(mine)
    xbuf[...] = jnp.zeros_like(xbuf)
    mkb[...] = jnp.zeros_like(mkb)

    barrier = pltpu.get_barrier_semaphore()

    def greet(rr, others_only):
        for k in range(D):
            for other in range(2):
                if others_only and k == 0 and other == 0:
                    continue
                pl.semaphore_signal(
                    barrier,
                    inc=1,
                    device_id={
                        "rows": rr,
                        "dates": lax.rem(d + k, D),
                        "cols": cp if other else c,
                    },
                    device_id_type=pl.DeviceIdType.MESH,
                )

    greet(r, True)

    @pl.when(r > 0)
    def _():
        greet(r - 1, False)

    @pl.when(r < R - 1)
    def _():
        greet(r + 1, False)

    turned = dot_tn(img_ref[...], perm_ref[...]).astype(BF)
    for hb in range(2):
        mine[hb] = turned[:, hb * 128 : (hb + 1) * 128]
        xbuf[d, 1 + hb, SIDE : SIDE + wdev, :] = turned[:, hb * 128 : (hb + 1) * 128]
    src_side = pl.multiple_of(cp * (wdev - SIDE), SIDE)
    dst_side = pl.multiple_of(c * (wdev + SIDE), SIDE)
    msrc_side = pl.multiple_of(128 + cp * (wdev - 128), 128)
    mdst_side = pl.multiple_of(c * (wdev + 128), 128)

    def image_copy(kind, src_d, dst_d, rr, sd):
        side = kind % 2
        where = kind // 2
        if where == 0:
            blocks, dst_blocks = pl.ds(0, 2), pl.ds(1, 2)
        elif where == 1:
            blocks, dst_blocks = pl.ds(0, 1), pl.ds(3, 1)
        else:
            blocks, dst_blocks = pl.ds(1, 1), pl.ds(0, 1)
        if side:
            a, b = pl.ds(src_side, SIDE), pl.ds(dst_side, SIDE)
        else:
            a, b = pl.ds(0, wdev), pl.ds(SIDE, wdev)
        return pltpu.make_async_remote_copy(
            src_ref=mine.at[blocks, a, :],
            dst_ref=xbuf.at[src_d, dst_blocks, b, :],
            send_sem=send_sem.at[kind * D + sd],
            recv_sem=recv_sem.at[kind * D + src_d],
            device_id={"rows": rr, "dates": dst_d, "cols": cp if side else c},
            device_id_type=pl.DeviceIdType.MESH,
        )

    def mask_copy(kind, to):
        side = kind % 2
        where = kind // 2
        if where == 0:
            a, b = pl.ds(1, own), pl.ds(1, own)
        elif where == 1:
            a, b = pl.ds(1, 1), pl.ds(own + 1, 1)
        else:
            a, b = pl.ds(own, 1), pl.ds(0, 1)
        if side:
            x, y = pl.ds(msrc_side, 128), pl.ds(mdst_side, 128)
        else:
            x, y = pl.ds(128, wdev), pl.ds(128, wdev)
        return pltpu.make_async_remote_copy(
            src_ref=mkb.at[a, :, x],
            dst_ref=mkb.at[b, :, y],
            send_sem=mask_send.at[kind],
            recv_sem=mask_recv.at[kind],
            device_id={"rows": to // D, "dates": lax.rem(to, D), "cols": cp if side else c},
            device_id_type=pl.DeviceIdType.MESH,
        )

    def needs_next(q):
        return own * q + own + 4 > strip

    def needs_prev(q):
        return own * q < 4

    greeted = 2 * D - 1 + 2 * D * ((r > 0).astype(jnp.int32) + (r < R - 1).astype(jnp.int32))
    pl.semaphore_wait(barrier, greeted)

    def sends(act):
        @pl.when(r > 0)
        def _():
            for k in range(D):
                to = lax.rem(d + k, D)

                @pl.when(needs_next(to))
                def _():
                    act(image_copy(2, d, to, r - 1, k))
                    act(image_copy(3, d, to, r - 1, k))

        @pl.when(r < R - 1)
        def _():
            for k in range(D):
                to = lax.rem(d + k, D)

                @pl.when(needs_prev(to))
                def _():
                    act(image_copy(4, d, to, r + 1, k))
                    act(image_copy(5, d, to, r + 1, k))

        for k in range(D):
            to = lax.rem(d + k, D)
            act(image_copy(1, d, to, r, k))
            if k > 0:
                act(image_copy(0, d, to, r, k))

    def mask_sends(act):
        act(mask_copy(1, f))

        @pl.when(f > 0)
        def _():
            act(mask_copy(2, f - 1))
            act(mask_copy(3, f - 1))

        @pl.when(f < R * D - 1)
        def _():
            act(mask_copy(4, f + 1))
            act(mask_copy(5, f + 1))

    sends(lambda copy: copy.start())
    date_no = lax.broadcasted_iota(jnp.int32, (T, wdev), 0)
    for row in range(own):
        rows = [
            cloud_ref[:, row, :].astype(F32),
            jnp.where(date_no >= counts_ref[row : row + 1, :], 1.0, 0.0).astype(F32),
        ]
        if 2 * T < 16:
            rows.append(jnp.zeros((16 - 2 * T, wdev), F32))
        mkb[1 + row, :, 128 : 128 + wdev] = jnp.concatenate(rows, axis=0).astype(BF)

    mask_sends(lambda copy: copy.start())

    def arrived(k):
        source = lax.rem(d + k, D)
        image_copy(1, source, d, r, k).wait_recv()
        if k > 0:
            image_copy(0, source, d, r, k).wait_recv()

        @pl.when((r < R - 1) & needs_next(d))
        def _():
            image_copy(2, source, d, r, k).wait_recv()
            image_copy(3, source, d, r, k).wait_recv()

        @pl.when((r > 0) & needs_prev(d))
        def _():
            image_copy(4, source, d, r, k).wait_recv()
            image_copy(5, source, d, r, k).wait_recv()

    k1[...] = jnp.zeros_like(k1)
    for off in range(4):
        for dy in range(3):
            for dx in range(3):
                for o in range(2):
                    row = 2 * off + o + dy
                    at = (row // 8) * 384 + dx * 128 + (row % 8) * 16
                    k1[off, at : at + bands, o * 128 : (o + 1) * 128] = w1_ref[dy, dx]
    for w_ref, k_ref in ((w2_ref, k2), (w3_ref, k3), (wdec_ref, kd)):
        k_ref[...] = jnp.zeros_like(k_ref)
        for dy in range(3):
            for dx in range(3):
                for o in range(2):
                    at = (o + dy) * 384 + dx * 128
                    k_ref[at : at + 128, o * 128 : (o + 1) * 128] = w_ref[dy, dx]

    even = lax.broadcasted_iota(jnp.int32, (1, model), 1) % 2 == 0
    for t in range(T):
        angle = day_ref[t].astype(F32) * freq_ref[...]
        pos_ref[t : t + 1, :] = jnp.where(even, jnp.sin(angle), jnp.cos(angle))
    hk = wkey_ref.shape[0]
    key_size = hk // heads

    def exact(a, b, dims):
        return lax.dot_general(
            a, b, (dims, ((), ())), precision=lax.Precision.HIGHEST, preferred_element_type=F32
        )

    owner = lax.broadcasted_iota(jnp.int32, (hk, heads), 0) // key_size
    owner = jnp.where(owner == lax.broadcasted_iota(jnp.int32, (hk, heads), 1), 1.0, 0.0)
    each = exact(owner.astype(F32), query_ref[...], ((1,), (1,)))
    place = lax.broadcasted_iota(jnp.int32, (hk, key_size), 0) % key_size
    place = place == lax.broadcasted_iota(jnp.int32, (hk, key_size), 1)
    column = jnp.sum(jnp.where(place, each, 0.0), axis=1, keepdims=True)
    pick = lax.broadcasted_iota(jnp.int32, (hk, 2 * L), 0) // key_size
    pick = pick == lax.broadcasted_iota(jnp.int32, (hk, 2 * L), 1) % heads
    q = jnp.where(pick, column * (1.0 / math.sqrt(key_size)), 0.0)
    full = exact(wkey_ref[...].astype(F32), q, ((0,), (0,)))
    folded = exact(win_ref[...].astype(F32), full, ((1,), (0,)))
    high = folded.astype(BF).astype(F32)
    lane = lax.broadcasted_iota(jnp.int32, folded.shape, 1)
    both = jnp.where(lane < L, high, folded - high)
    chan = folded.shape[0]
    for t in range(T):
        ws[t * chan : (t + 1) * chan, :] = jnp.where((lane % L) // heads == t, both, 0.0).astype(BF)
    shift = exact(pos_ref[...], full, ((1,), (0,)))
    lane_t = (lax.broadcasted_iota(jnp.int32, shift.shape, 1) % L) // heads
    shift = jnp.where(lane_t == lax.broadcasted_iota(jnp.int32, shift.shape, 0), shift, 0.0)
    posr_ref[...] = jnp.sum(shift, axis=0, keepdims=True)

    kk = lax.broadcasted_iota(jnp.int32, (512, 256), 0)
    nn = lax.broadcasted_iota(jnp.int32, (512, 256), 1)
    same = ((kk // 128) * 4 + (kk % 64) // 16 == d * own + nn // 16) & (kk % 16 == nn % 16)
    for p in range(dl):
        sel[p] = jnp.where(same & ((kk % 128) // 64 == p), 1.0, 0.0).astype(BF)

    px = lax.broadcasted_iota(jnp.int32, (M, 128), 0)
    at_col = px + (c * wdev - SIDE)
    inside = (at_col >= 0) & (at_col < 2 * wdev)
    col_mask = jnp.where(inside, 1.0, 0.0).astype(F32)
    first_row = r * strip + d * own

    def row_mask(rel):
        at = first_row + rel
        ok = ((at >= 0) & (at < height)).astype(F32)
        return ok

    def spread(y, into, base, rel):
        y = y * (col_mask * row_mask(rel))
        into[:, pl.ds(base, 128)] = pltpu.roll(y, 1, 0).astype(BF)
        into[:, pl.ds(base + 128, 128)] = y.astype(BF)
        into[:, pl.ds(base + 256, 128)] = pltpu.roll(y, M - 1, 0).astype(BF)

    def one_date(i, carry):
        t = lax.rem(d * dl + i, T)
        source = t // dl
        par = lax.rem(t, dl)
        window = dot(xbuf[source, 0], sel[par, 0:128, :])
        for b in range(1, 4):
            window = window + dot(xbuf[source, b], sel[par, b * 128 : (b + 1) * 128, :])
        for h in range(2):
            part = window[:, h * 128 : (h + 1) * 128]
            xw[:, h * 384 : h * 384 + 128] = pltpu.roll(part, 1, 0).astype(BF)
            xw[:, h * 384 + 128 : h * 384 + 256] = part.astype(BF)
            xw[:, h * 384 + 256 : h * 384 + 384] = pltpu.roll(part, M - 1, 0).astype(BF)
        for j in range((own + 6) // 2):
            at = (j // 4) * 384
            if j % 4 == 3:
                y = dot(xw[...], k1[3])
            else:
                y = dot(xw[:, at : at + 384], k1[j % 4, 0:384, :])
            for o in range(2):
                v = jnp.maximum(y[:, o * 128 : (o + 1) * 128] + b1_ref[...], 0.0)
                spread(v, s1, (2 * j + o) * 384, 2 * j + o - 3)
        for j in range((own + 4) // 2):
            y = dot(s1[:, j * 768 : j * 768 + 1536], k2[...])
            for o in range(2):
                v = jnp.maximum(y[:, o * 128 : (o + 1) * 128] + b2_ref[...], 0.0)
                spread(v, s2, (2 * j + o) * 384, 2 * j + o - 2)
        for j in range((own + 2) // 2):
            y = dot(s2[:, j * 768 : j * 768 + 1536], k3[...])
            for o in range(2):
                v = jnp.maximum(y[:, o * 128 : (o + 1) * 128] + b3_ref[...], 0.0)
                enc[2 * j + o, :, pl.ds(pl.multiple_of(t * 128, 128), 128)] = v.astype(BF)
        return carry

    for k in range(D):
        arrived(k)
        lax.fori_loop(k * dl, (k + 1) * dl, one_date, 0)

    mask_copy(1, f).wait_recv()

    @pl.when(f < R * D - 1)
    def _():
        mask_copy(2, f).wait_recv()
        mask_copy(3, f).wait_recv()

    @pl.when(f > 0)
    def _():
        mask_copy(4, f).wait_recv()
        mask_copy(5, f).wait_recv()

    for i in range(own + 2):
        z = dot(enc[i], ws[...])
        for t in range(T):
            v = dot(enc[i, :, t * 128 : (t + 1) * 128], win_ref[...]) + pos_ref[t : t + 1, :]
            pa[i % 2, :, t * model : (t + 1) * model] = v.astype(BF)
        raw = z + pltpu.roll(z, L, 1) + posr_ref[...]
        extra = dot_tn(mkb[i], bsel_ref[...])[128 - SIDE : 128 + wdev + SIDE]
        w = jnp.exp(8.0 * jnp.tanh(raw * 0.125) + extra)
        total = w
        step = heads
        while step < L:
            total = total + pltpu.roll(total, step, 1)
            step *= 2
        att = (w / total).astype(BF)
        pooled = None
        for t in range(T):
            cols = slice(t * model, (t + 1) * model)
            term = dot(att, ex_ref[:, cols]) * pa[i % 2, :, cols].astype(F32)
            pooled = term if pooled is None else pooled + term
        v = jnp.maximum(dot(pooled.astype(BF), wmlp_ref[...]) + bmlp_ref[...], 0.0)
        spread(v, s3, i * 384, i - 1)

    for j in range(own // 2):
        y = dot(s3[:, j * 768 : j * 768 + 1536], kd[...])
        for o in range(2):
            v = jnp.maximum(y[SIDE : SIDE + wdev, o * 128 : (o + 1) * 128] + bdec_ref[...], 0.0)
            out_ref[:, 2 * j + o, :] = dot_nt(wout_ref[...], v.astype(BF))

    sends(lambda copy: copy.wait_send())
    mask_sends(lambda copy: copy.wait_send())


def on_device(
    axes,
    images,
    cloud_mask,
    counts,
    day_of_year,
    w_first,
    b_first,
    w_second,
    b_second,
    w_third,
    b_third,
    w_in,
    w_key,
    master_query,
    w_mlp,
    b_mlp,
    w_dec,
    b_dec,
    w_out,
    b_out,
):
    R, D = axes
    dl, bands, strip, wdev = images.shape
    own = counts.shape[0]
    T = cloud_mask.shape[0]
    heads, key_size = master_query.shape
    model = w_in.shape[1]
    L = T * heads
    M = wdev + 2 * SIDE
    chan = w_in.shape[0]
    cfg = (R, D, dl, own, strip, wdev, heads, model, bands)

    perm = np.zeros((dl * bands * strip, 256), np.float32)
    for p in range(dl):
        for ch in range(bands):
            for row in range(strip):
                lane = (row // 4) * 128 + p * 64 + (row % 4) * 16 + ch
                perm[(p * bands + ch) * strip + row, lane] = 1.0
    n = np.arange(2 * L)
    date_of = (n % L) // heads
    ex = np.zeros((2 * L, T * model), np.float32)
    for t in range(T):
        for m in range(model):
            ex[t * heads + m // (model // heads), t * model + m] = 1.0
    bsel = np.zeros((16, 2 * L), np.float32)
    for t in range(T):
        bsel[t, date_of == t] = -4.0
        bsel[T + t, date_of == t] = -1e30
    freq = np.power(1000.0, -2.0 * (np.arange(model) // 2) / model).astype(np.float32)[None]

    args = (
        images.reshape(dl * bands * strip, wdev),
        cloud_mask,
        counts,
        day_of_year,
        jnp.asarray(freq),
        jnp.asarray(perm, BF),
        w_first,
        b_first[None],
        w_second,
        b_second[None],
        w_third,
        b_third[None],
        w_in,
        w_key.T,
        master_query.T,
        jnp.asarray(ex, BF),
        jnp.asarray(bsel, BF),
        w_mlp,
        b_mlp[None],
        w_dec,
        b_dec[None],
        w_out,
    )
    specs = [pl.BlockSpec(memory_space=pltpu.VMEM)] * len(args)
    specs[3] = pl.BlockSpec(memory_space=pltpu.SMEM)
    out = pl.pallas_call(
        functools.partial(kernel, cfg),
        out_shape=jax.ShapeDtypeStruct((bands, own, wdev), F32),
        in_specs=specs,
        out_specs=pl.BlockSpec(memory_space=pltpu.VMEM),
        scratch_shapes=[
            pltpu.VMEM((2, wdev, 128), BF),
            pltpu.VMEM((D, 4, M, 128), BF),
            pltpu.VMEM((own + 2, 16, wdev + 256), BF),
            pltpu.VMEM((M, 768), BF),
            pltpu.VMEM((M, (own + 6) * 384), BF),
            pltpu.VMEM((M, (own + 4) * 384), BF),
            pltpu.VMEM((M, (own + 2) * 384), BF),
            pltpu.VMEM((own + 2, M, T * chan), BF),
            pltpu.VMEM((2, M, T * model), BF),
            pltpu.VMEM((4, 768, 256), BF),
            pltpu.VMEM((12 * chan, 2 * chan), BF),
            pltpu.VMEM((12 * chan, 2 * chan), BF),
            pltpu.VMEM((12 * chan, 2 * chan), BF),
            pltpu.VMEM((T * chan, 2 * L), BF),
            pltpu.VMEM((dl, 512, 256), BF),
            pltpu.VMEM((T, model), F32),
            pltpu.VMEM((1, 2 * L), F32),
            pltpu.SemaphoreType.DMA((6 * D,)),
            pltpu.SemaphoreType.DMA((6 * D,)),
            pltpu.SemaphoreType.DMA((6,)),
            pltpu.SemaphoreType.DMA((6,)),
        ],
        compiler_params=pltpu.CompilerParams(
            collective_id=0, has_side_effects=True, vmem_limit_bytes=56 * 1024 * 1024
        ),
    )(*args)
    return out + b_out[:, None, None]


def solution(mesh):
    placed = (
        P("dates", None, ("groups", "rows"), "cols"),
        P(None, ("groups", "rows", "dates"), "cols"),
        P(("groups", "rows", "dates"), "cols"),
        P("groups"),
    ) + (P(),) * 15
    return jax.shard_map(
        functools.partial(on_device, (mesh.shape["rows"], mesh.shape["dates"])),
        mesh=mesh,
        in_specs=placed,
        out_specs=P(None, ("groups", "rows", "dates"), "cols"),
        check_vma=False,
    )
```
